32 devices in a mesh: groups: 2 (over y), store: 4 (over x, core), tensor: 4 (over z).
Axes of the slice: x: 2, y: 2, z: 4, core: 2. Of those that a mesh axis runs over, the one named last changes fastest.
Arguments:
- hidden: bfloat16 [512, 8192], P(('groups', 'store', 'tensor')), parts along dimension 0, may hold values from -6 to 6
- queries: bfloat16 [512, 8192], P(('groups', 'store', 'tensor')), parts along dimension 0
- cached_key_rows: bfloat16 [512, 8, 128, 128], P(('groups', 'store', 'tensor')), parts along dimension 0
- cached_value_rows: bfloat16 [512, 8, 128, 128], P(('groups', 'store', 'tensor')), parts along dimension 0, may hold values from -6 to 6
- cache_length: int32 [512], P(('groups', 'store', 'tensor')), parts along dimension 0, may hold values from 2 to 128
- output_weight: bfloat16 [8192, 8192], P('tensor'), may hold values from -0.5 to 0.5
- shrink_matrices: bfloat16 [256, 64, 8192], P(('groups', 'store'), None, 'tensor'), parts along dimension 0, may hold values from -0.5 to 0.5
- expand_matrices: bfloat16 [256, 64, 8192], P(('groups', 'store'), 'tensor'), parts along dimension 0, may hold values from -0.75 to 0.75
- block_slot_rows: int32 [64, 16], P(('groups', 'store')), parts along dimension 0, may hold values from -1 to 63, as said below
- adapter_per_block: int32 [64], P(('groups', 'store')), parts along dimension 0, may hold values from 0 to 127, as said below
- adapter_store_slot: int32 [256], P('groups'), parts along dimension 0, may hold values from 0 to 127, as said below
Outputs:
- mixed: bfloat16 [512, 8192], P(('groups', 'store', 'tensor')), parts along dimension 0
The draws below stay inside these ranges and needn't reach their ends.
There are 2 independent parts, one for each index of `groups`. The reference program is written for one: setup_inputs(seed, part) draws one part's arguments, and reference() takes and returns one part's arrays. A program takes and returns all parts, laid end to end along the dimension named above; an argument that names none is the same for every part. Nothing has to cross between parts.
Inputs may be any that keep to these rules, and one draw needn't show every extreme that they name: `block_slot_rows`: every row of a sub-group stands in exactly one slot of that sub-group's blocks; empty slots hold -1. `adapter_per_block`: in every sub-group, at most 4 blocks name an adapter whose slot lies with one store index (slot // 32), and some store index has exactly 4. `adapter_store_slot`: A permutation.
All inputs are finite; a program needn't handle non-finite values.
Results may differ from the reference program's by a relative error of at most 0.013.
Values may be sent and summed in bfloat16 or wider, within the bound.
A program may use at most 192 MiB of HBM per device.

```python
import jax
import jax.numpy as jnp
from jax import lax

MODEL_WIDTH = 8192
QUERY_HEADS = 64
KVH = 8
HEAD_SIZE = 128
ADAPTER_RANK = 64
NBLK = 8
CACHE = 128
SLOTS_DEV = 32
GROUP_ROWS = 64
ROWS_ALL = 256
BLK = 16
ADAPTER_TOTAL = 128
N_STORE = 4


def ownership(key):
    slot_of = jax.random.permutation(jax.random.fold_in(key, 101), ADAPTER_TOTAL).astype(jnp.int32)
    holder = jnp.zeros((ADAPTER_TOTAL,), jnp.int32).at[slot_of].set(jnp.arange(ADAPTER_TOTAL, dtype=jnp.int32))
    capacity = NBLK // 2
    hot_owner = jax.random.randint(jax.random.fold_in(key, 102), (N_STORE, 1), 0, N_STORE)
    others = (hot_owner + 1 + jax.random.randint(jax.random.fold_in(key, 103), (N_STORE, NBLK - capacity), 0, N_STORE - 1)) % N_STORE
    owners = jnp.concatenate([jnp.broadcast_to(hot_owner, (N_STORE, capacity)), others], axis=1)
    owners = jax.random.permutation(jax.random.fold_in(key, 104), owners, axis=1, independent=True)
    first_pick = jax.random.randint(jax.random.fold_in(key, 105), (N_STORE, NBLK), 0, SLOTS_DEV)
    second_pick = jax.random.randint(jax.random.fold_in(key, 106), (N_STORE, NBLK), 0, SLOTS_DEV)
    local_slot = jnp.minimum(first_pick, second_pick)
    adapters = holder[owners * SLOTS_DEV + local_slot]
    return (slot_of, adapters.reshape(N_STORE * NBLK).astype(jnp.int32))


def key_table(key, amount):
    table = jax.random.normal(jax.random.fold_in(key, 201), (ROWS_ALL, KVH, CACHE, HEAD_SIZE), jnp.float32)
    row_ids = jnp.arange(ROWS_ALL)
    strength = 12.0 * (1.0 + (row_ids // 4 % 3).astype(jnp.float32))
    aligned = (row_ids % 4 == 0).astype(jnp.float32) * amount
    second = (1.0 - aligned[:, None, None, None]) * table[:, :, 1:2, :]
    table = jnp.concatenate([table[:, :, 0:1, :], second, table[:, :, 2:, :]], axis=2)
    return (table, strength, aligned)


def draw_adapter_store_slot(key, part):
    shared = ownership(key)
    return shared[0]


def draw_adapter_per_block(key, part):
    shared = ownership(key)
    return shared[1]


def draw_block_slot_rows(key, part):
    key = jax.random.fold_in(key, 5)
    half_blocks = NBLK // 2
    spread = jax.random.randint(jax.random.fold_in(key, 1), (N_STORE, half_blocks), -(BLK // 2), BLK // 2 + 1)
    spread = spread.at[:, 0].set(BLK // 2)
    counts = BLK // 2 + jnp.concatenate([spread, -spread], axis=1)
    counts = jax.random.permutation(jax.random.fold_in(key, 2), counts, axis=1, independent=True)
    starts = jnp.cumsum(counts, axis=1) - counts
    shuffled = jax.random.permutation(jax.random.fold_in(key, 3), jnp.broadcast_to(jnp.arange(GROUP_ROWS, dtype=jnp.int32), (N_STORE, GROUP_ROWS)), axis=1, independent=True)
    places = jnp.arange(BLK, dtype=jnp.int32)
    reach = jnp.minimum(starts[:, :, None] + places[None, None, :], GROUP_ROWS - 1)
    picked = shuffled[jnp.arange(N_STORE)[:, None, None], reach]
    listed = jnp.where(places[None, None, :] < counts[:, :, None], picked, -1)
    return listed.reshape(N_STORE * NBLK, BLK).astype(jnp.int32)


def draw_cache_length(key, part):
    key = jax.random.fold_in(key, 6)
    lengths = jax.random.randint(jax.random.fold_in(key, 1), (ROWS_ALL,), 2, CACHE + 1)
    chosen = jax.random.randint(jax.random.fold_in(key, 2), (), 0, ROWS_ALL)
    return lengths.at[chosen].set(CACHE).astype(jnp.int32)


def draw_cached_key_rows(key, part):
    shared = key_table(key, 0.0)
    return shared[0].astype(jnp.bfloat16)


def draw_queries(key, part):
    shared = key_table(key, 0.0)
    table, strength, aligned = shared
    key = jax.random.fold_in(key, 8)
    drawn = jax.random.normal(key, (ROWS_ALL, QUERY_HEADS * HEAD_SIZE), jnp.float32)
    return ((1.0 - aligned[:, None]) * drawn).astype(jnp.bfloat16)


def levels(key, extent, cuts, low, largest):
    def one(axis_at, parts):
        heights = jax.random.uniform(jax.random.fold_in(jax.random.fold_in(key, 6), axis_at), (parts,), jnp.float32, low / len(cuts), largest / len(cuts))
        return jnp.repeat(jnp.exp(heights), extent[axis_at] // parts).reshape((-1,) + (1,) * (len(extent) - axis_at - 1))

    level = one(*cuts[0])
    for cut in cuts[1:]:
        level = level * one(*cut)
    return level


def scatter_about(stream_key, shape, scale, most, pieces=(), kind=jnp.bfloat16):
    values = jax.random.normal(stream_key, shape, jnp.float32) * scale
    if len(pieces) > 0:
        values = levels(stream_key, shape, pieces, -0.22, 0.18) * values
    return jnp.clip(values, min=-most, max=most).astype(kind)


def setup_inputs(seed: int = 0, part: int = 0) -> dict:
    seeds = jax.random.split(jax.random.key(seed), 12)
    part_splits = jax.random.split(jax.random.fold_in(seeds[11], part), 12)
    hidden = scatter_about(part_splits[0], (ROWS_ALL, MODEL_WIDTH), 1.0, 6.0, ((0, 16),))
    queries = draw_queries(jax.random.fold_in(jax.random.fold_in(seeds[11], part), 71), part)
    cached_key_rows = draw_cached_key_rows(jax.random.fold_in(jax.random.fold_in(seeds[11], part), 71), part)
    cached_value_rows = scatter_about(part_splits[3], (ROWS_ALL, KVH, CACHE, HEAD_SIZE), 1.0, 6.0, ((0, 16),))
    cache_length = draw_cache_length(jax.random.fold_in(jax.random.fold_in(seeds[11], part), 71), part)
    output_weight = scatter_about(seeds[5], (QUERY_HEADS * HEAD_SIZE, MODEL_WIDTH), (QUERY_HEADS * HEAD_SIZE // 64) ** -0.5, 0.5, ((0, 4),))
    shrink_matrices = scatter_about(part_splits[6], (ADAPTER_TOTAL, ADAPTER_RANK, QUERY_HEADS * HEAD_SIZE), (QUERY_HEADS * HEAD_SIZE // 64) ** -0.5, 0.5, ((0, 4), (2, 4)))
    expand_matrices = scatter_about(part_splits[7], (ADAPTER_TOTAL, ADAPTER_RANK, MODEL_WIDTH), ADAPTER_RANK ** -0.5, 0.75, ((0, 4), (1, 4)))
    block_slot_rows = draw_block_slot_rows(jax.random.fold_in(jax.random.fold_in(seeds[11], part), 71), part)
    adapter_per_block = draw_adapter_per_block(jax.random.fold_in(jax.random.fold_in(seeds[11], part), 71), part)
    adapter_store_slot = draw_adapter_store_slot(jax.random.fold_in(jax.random.fold_in(seeds[11], part), 71), part)
    return {"hidden": hidden, "queries": queries, "cached_key_rows": cached_key_rows, "cached_value_rows": cached_value_rows, "cache_length": cache_length, "output_weight": output_weight, "shrink_matrices": shrink_matrices, "expand_matrices": expand_matrices, "block_slot_rows": block_slot_rows, "adapter_per_block": adapter_per_block, "adapter_store_slot": adapter_store_slot}


ADAPTER_SCALE = 2.0


def attend(queries, cached_key_rows, cached_value_rows, cache_length):
    rows_all = queries.shape[0]
    grouped = queries.astype(jnp.float32).reshape(rows_all, KVH, QUERY_HEADS // KVH, HEAD_SIZE)
    scores = jnp.einsum("rkgd,rkpd->rkgp", grouped, cached_key_rows.astype(jnp.float32)) * (HEAD_SIZE ** -0.5)
    live_pos = jnp.arange(CACHE, dtype=jnp.int32)[None, :] < cache_length[:, None]
    scores = jnp.where(live_pos[:, None, None, :], scores, -jnp.inf)
    highest = jnp.max(scores, axis=-1, keepdims=True)
    raised = jnp.exp(scores - highest)
    weights = (raised / jnp.sum(raised, axis=-1, keepdims=True)).astype(jnp.bfloat16)
    outputs = jnp.einsum("rkgp,rkpd->rkgd", weights.astype(jnp.float32), cached_value_rows.astype(jnp.float32))
    return outputs.astype(jnp.bfloat16).reshape(rows_all, QUERY_HEADS * HEAD_SIZE)


def reference(hidden, queries, cached_key_rows, cached_value_rows, cache_length, output_weight, shrink_matrices, expand_matrices, block_slot_rows, adapter_per_block, adapter_store_slot):
    attended = attend(queries, cached_key_rows, cached_value_rows, cache_length)
    base = jnp.dot(attended, output_weight, preferred_element_type=jnp.float32)
    block_count = block_slot_rows.shape[0] // N_STORE
    owner_group = jnp.arange(block_slot_rows.shape[0], dtype=jnp.int32) // block_count
    targets = jnp.where(block_slot_rows >= 0, block_slot_rows + (owner_group * GROUP_ROWS)[:, None], ROWS_ALL).astype(jnp.int32)
    block_slot = adapter_store_slot[adapter_per_block].astype(jnp.int32)
    row_slot = jnp.zeros((ROWS_ALL + 1,), jnp.int32).at[targets].set(jnp.broadcast_to(block_slot[:, None], block_slot_rows.shape))[:ROWS_ALL]

    def row_delta(item):
        row_number, row_place = item
        shrink_output = jnp.dot(shrink_matrices[row_place], row_number, preferred_element_type=jnp.float32).astype(jnp.bfloat16)
        return ADAPTER_SCALE * jnp.dot(shrink_output, expand_matrices[row_place], preferred_element_type=jnp.float32)

    delta = lax.map(row_delta, (attended, row_slot))
    return (hidden.astype(jnp.float32) + base + delta).astype(jnp.bfloat16)
```

```python
import functools

import jax
import jax.numpy as jnp
from jax import lax
from jax.experimental import pallas as pl
from jax.experimental.pallas import tpu as pltpu
from jax.sharding import PartitionSpec as P

ADAPTER_SCALE = 2.0
MESH = pl.DeviceIdType.MESH
CHUNKS = 8
WEIGHT_SLOTS = 4
VMEM_BYTES = 60 * 1024 * 1024


def attend_kernel(length_ref, q_ref, k_ref, v_ref, out_ref):
    rows, kv_heads, positions, head_dim = k_ref.shape
    step = pl.program_id(0)
    place = lax.broadcasted_iota(jnp.int32, (1, 1, positions), 2)
    for row in range(rows):
        q = q_ref[row].reshape(kv_heads, -1, head_dim)
        scores = lax.dot_general(
            q, k_ref[row], (((2,), (2,)), ((0,), (0,))), preferred_element_type=jnp.float32
        ) * head_dim ** (-0.5)
        scores = jnp.where(place < length_ref[step * rows + row], scores, -jnp.inf)
        highest = jnp.max(scores, axis=-1, keepdims=True)
        raised = jnp.exp(scores - highest)
        weights = (raised / jnp.sum(raised, axis=-1, keepdims=True)).astype(jnp.bfloat16)
        outputs = lax.dot_general(
            weights, v_ref[row], (((2,), (1,)), ((0,), (0,))), preferred_element_type=jnp.float32
        )
        out_ref[row] = outputs.astype(jnp.bfloat16).reshape(-1, head_dim)


def attend_rows(queries, cached_key_rows, cached_value_rows, cache_length):
    rows_dev, kv_heads, positions, head_dim = cached_key_rows.shape
    heads = queries.shape[1] // head_dim
    rows = 2 if rows_dev % 2 == 0 else 1
    cache_spec = pl.BlockSpec((rows, kv_heads, positions, head_dim), lambda i, n: (i, 0, 0, 0))
    head_spec = pl.BlockSpec((rows, heads, head_dim), lambda i, n: (i, 0, 0))
    return pl.pallas_call(
        attend_kernel,
        grid_spec=pltpu.PrefetchScalarGridSpec(
            num_scalar_prefetch=1,
            grid=(rows_dev // rows,),
            in_specs=[head_spec, cache_spec, cache_spec],
            out_specs=head_spec,
        ),
        out_shape=jax.ShapeDtypeStruct((rows_dev, heads, head_dim), jnp.bfloat16),
        compiler_params=pltpu.CompilerParams(vmem_limit_bytes=24 * 1024 * 1024),
    )(cache_length, queries.reshape(rows_dev, heads, head_dim), cached_key_rows, cached_value_rows)


def project_kernel(
    att_ref,
    slot_ref,
    hidden_ref,
    weight_hbm,
    shrink_hbm,
    expand_hbm,
    out_ref,
    rows_ref,
    slots_ref,
    weight_ref,
    shrink_ref,
    expand_ref,
    base_ref,
    part_ref,
    part_recv,
    mix_ref,
    delta_ref,
    near_recv,
    far_send,
    far_recv,
    line_send,
    line_recv,
    load_sem,
    weight_sem,
    turn_sem,
    rows_sem,
    slots_sem,
    part_sem,
    near_sem,
    far_sem,
    line_sem,
):
    store = lax.axis_index("store")
    tensor = lax.axis_index("tensor")
    tensors = lax.axis_size("tensor")
    stores = lax.axis_size("store")
    near = store + 1 - 2 * (store % 2)
    far = (store + 2) % 4
    cross = (near + 2) % 4
    slots_dev, rank, width = shrink_ref.shape
    portion = expand_ref.shape[1]
    rows_dev = att_ref.shape[1]
    group_rows = tensors * rows_dev
    rows_all = stores * group_rows
    chunk = weight_ref.shape[2]

    def line(step):
        return lax.rem(tensor + step, tensors)

    barrier = pltpu.get_barrier_semaphore()
    for step in range(1, tensors):
        pl.semaphore_signal(barrier, inc=1, device_id={"tensor": line(step)}, device_id_type=MESH)
    for other in (near, far, cross):
        pl.semaphore_signal(barrier, inc=1, device_id={"store": other}, device_id_type=MESH)
    shrink_load = pltpu.make_async_copy(shrink_hbm, shrink_ref, load_sem.at[0])
    expand_load = pltpu.make_async_copy(expand_hbm, expand_ref, load_sem.at[1])

    def weight_load(j):
        return pltpu.make_async_copy(
            weight_hbm.at[:, pl.ds(pl.multiple_of(j * chunk, chunk), chunk)],
            weight_ref.at[lax.rem(j, WEIGHT_SLOTS)],
            weight_sem.at[lax.rem(j, WEIGHT_SLOTS)],
        )

    for j in range(2):
        weight_load(j).start()
    shrink_load.start()
    for j in range(2, WEIGHT_SLOTS):
        weight_load(j).start()
    expand_load.start()
    slots_ref[store] = slot_ref[...]
    pl.semaphore_wait(barrier, tensors - 1 + 3)

    def remote(src, dst, sems, at, **where):
        return pltpu.make_async_remote_copy(
            src_ref=src,
            dst_ref=dst,
            send_sem=sems.at[(0,) + at],
            recv_sem=sems.at[(1,) + at],
            device_id=where,
            device_id_type=MESH,
        )

    turns = [
        remote(att_ref.at[line(step)], rows_ref.at[store, tensor], turn_sem, (step,), tensor=line(step))
        for step in range(1, tensors)
    ]
    for copy in turns:
        copy.start()
    rows_ref[store, tensor] = att_ref[tensor]

    slot_copies = [
        remote(slots_ref.at[store], slots_ref.at[store], slots_sem, (i,), store=other)
        for i, other in enumerate((near, far, cross))
    ]
    for copy in slot_copies:
        copy.start()

    def share(step):
        block = rows_ref.at[store, lax.rem(tensor + tensors - step, tensors)]
        return [
            remote(block, block, rows_sem, (0, step), store=far),
            remote(block, block, rows_sem, (1, step), store=near),
        ]

    shares = [share(step) for step in range(tensors)]
    for step in range(tensors):
        if step > 0:
            turns[step - 1].wait_recv()
        for copy in shares[step]:
            copy.start()

    own_rows = rows_ref.at[store]

    def project(j, _):
        weight_load(j).wait()
        base_ref[j] = jnp.dot(
            own_rows[...].reshape(group_rows, width),
            weight_ref[lax.rem(j, WEIGHT_SLOTS)],
            preferred_element_type=jnp.float32,
        )
        return 0

    relays = []
    for step in range(tensors):
        block = rows_ref.at[far, lax.rem(tensor + tensors - step, tensors)]
        relays.append(remote(block, block, rows_sem, (2, step), store=near))

    lax.fori_loop(0, 2, project, 0)
    for step in range(tensors):
        shares[step][0].wait_recv()
        relays[step].start()
    lax.fori_loop(2, WEIGHT_SLOTS, project, 0)
    for j in range(WEIGHT_SLOTS, min(2 * WEIGHT_SLOTS, CHUNKS)):
        weight_load(j).start()
    for copy in slot_copies:
        copy.wait_recv()
    for step in range(tensors):
        shares[step][1].wait_recv()
        relays[step].wait_recv()
    shrink_load.wait()

    slot_row = jnp.max(jnp.max(slots_ref[...], axis=0), axis=0, keepdims=True) - store * slots_dev
    batch = 4
    part_ref[...] = jnp.zeros_like(part_ref)

    def shrink_step(i, _):
        first = i * batch
        product = lax.dot_general(
            shrink_ref[pl.ds(first, batch)].reshape(batch * rank, width),
            rows_ref[...].reshape(rows_all, width),
            (((1,), (1,)), ((), ())),
            preferred_element_type=jnp.float32,
        ).reshape(batch, rank, rows_all)
        total = jnp.zeros((rank, rows_all), jnp.float32)
        for b in range(batch):
            total += jnp.where(slot_row == first + b, product[b], 0.0)
        part_ref[...] += total.reshape(part_ref.shape)
        return 0

    lax.fori_loop(0, slots_dev // batch, shrink_step, 0)
    parts = [
        remote(part_ref.at[line(step)], part_recv.at[step - 1], part_sem, (step,), tensor=line(step))
        for step in range(1, tensors)
    ]
    for copy in parts:
        copy.start()
    lax.fori_loop(WEIGHT_SLOTS, CHUNKS, project, 0)
    shrunk = part_ref[tensor]
    for step in range(1, tensors):
        parts[step - 1].wait_recv()
        shrunk += part_recv[step - 1]
    shrunk = ADAPTER_SCALE * shrunk.astype(jnp.bfloat16).astype(jnp.float32)
    slot_ids = lax.broadcasted_iota(jnp.int32, (slots_dev, portion, rows_all), 0)
    spread = jnp.where(slot_row[None] == slot_ids, shrunk[None], 0.0)
    mix_ref[...] = spread.reshape(slots_dev * portion, rows_all).T.astype(jnp.bfloat16)
    expand_load.wait()

    def near_copies(j):
        return [
            remote(delta_ref.at[j, near], near_recv.at[j, 0], near_sem, (0, j), store=near),
            remote(delta_ref.at[j, cross], near_recv.at[j, 1], near_sem, (1, j), store=near),
        ]

    def far_copy(j):
        return remote(far_send.at[j], far_recv.at[j], far_sem, (j,), store=far)

    def line_copies(j):
        return [
            remote(
                line_send.at[j, line(step)], line_recv.at[j, step - 1], line_sem, (step, j), tensor=line(step)
            )
            for step in range(1, tensors)
        ]

    def columns(j):
        return pl.ds(pl.multiple_of(j * chunk, chunk), chunk)

    def send_far(j):
        near_copies(j)[1].wait_recv()
        total = delta_ref[j, far].astype(jnp.float32) + near_recv[j, 1].astype(jnp.float32)
        far_send[j] = total.astype(jnp.bfloat16)
        far_copy(j).start()

    def expand_step(j, _):
        delta_ref[j] = (
            jnp.dot(
                mix_ref[...],
                expand_ref[:, :, columns(j)].reshape(slots_dev * portion, chunk),
                preferred_element_type=jnp.float32,
            )
            .astype(jnp.bfloat16)
            .reshape(stores, group_rows, chunk)
        )
        for copy in reversed(near_copies(j)):
            copy.start()

        @pl.when(j > 0)
        def _():
            send_far(j - 1)

        return 0

    lax.fori_loop(0, CHUNKS, expand_step, 0)
    send_far(CHUNKS - 1)

    def line_step(j, _):
        near_copies(j)[0].wait_recv()
        far_copy(j).wait_recv()
        total = (
            base_ref[j]
            + delta_ref[j, store].astype(jnp.float32)
            + near_recv[j, 0].astype(jnp.float32)
            + far_recv[j].astype(jnp.float32)
        )
        line_send[j] = total.astype(jnp.bfloat16).reshape(tensors, rows_dev, chunk)
        for copy in line_copies(j):
            copy.start()
        return 0

    lax.fori_loop(0, CHUNKS, line_step, 0)

    def last_step(j, _):
        total = hidden_ref[:, columns(j)].astype(jnp.float32) + line_send[j, tensor].astype(jnp.float32)
        for step, copy in enumerate(line_copies(j)):
            copy.wait_recv()
            total += line_recv[j, step].astype(jnp.float32)
        out_ref[:, columns(j)] = total.astype(jnp.bfloat16)
        return 0

    lax.fori_loop(0, CHUNKS, last_step, 0)

    for copy in turns + slot_copies + relays + parts:
        copy.wait_send()
    for pair in shares:
        for copy in pair:
            copy.wait_send()

    def drain(j, _):
        for copy in near_copies(j) + [far_copy(j)] + line_copies(j):
            copy.wait_send()
        return 0

    lax.fori_loop(0, CHUNKS, drain, 0)


def rows_plan(
    hidden,
    queries,
    cached_key_rows,
    cached_value_rows,
    cache_length,
    output_weight,
    shrink_matrices,
    expand_matrices,
    block_slot_rows,
    adapter_per_block,
    adapter_store_slot,
):
    tensors = lax.axis_size("tensor")
    stores = lax.axis_size("store")
    rows_dev, model = hidden.shape
    width = output_weight.shape[0]
    slots_dev, rank, _ = shrink_matrices.shape
    portion = expand_matrices.shape[1]
    group_rows = tensors * rows_dev
    rows_all = stores * group_rows
    chunk = model // CHUNKS

    attended = attend_rows(queries, cached_key_rows, cached_value_rows, cache_length)
    att = attended.reshape(rows_dev, tensors, width).transpose(1, 0, 2)

    slot_of = adapter_store_slot[adapter_per_block]
    row_ids = jnp.arange(rows_all, dtype=jnp.int32) - lax.axis_index("store") * group_rows
    listed = block_slot_rows[:, :, None] == row_ids
    own_slots = jnp.max(jnp.where(listed, slot_of[:, None, None], -1), axis=(0, 1))
    in_group = (row_ids >= 0) & (row_ids < group_rows)
    own_slots = jnp.broadcast_to(jnp.where(in_group, own_slots, -1), (8, rows_all))

    vmem = pl.BlockSpec(memory_space=pltpu.VMEM)
    hbm = pl.BlockSpec(memory_space=pl.ANY)
    bf16, f32 = jnp.bfloat16, jnp.float32
    dma = pltpu.SemaphoreType.DMA
    return pl.pallas_call(
        project_kernel,
        out_shape=jax.ShapeDtypeStruct((rows_dev, model), bf16),
        in_specs=[vmem, vmem, vmem, hbm, hbm, hbm],
        out_specs=vmem,
        scratch_shapes=[
            pltpu.VMEM((stores, tensors, rows_dev, width), bf16),
            pltpu.VMEM((stores, 8, rows_all), jnp.int32),
            pltpu.VMEM((WEIGHT_SLOTS, width, chunk), bf16),
            pltpu.VMEM((slots_dev, rank, width), bf16),
            pltpu.VMEM((slots_dev, portion, model), bf16),
            pltpu.VMEM((CHUNKS, group_rows, chunk), f32),
            pltpu.VMEM((tensors, portion, rows_all), f32),
            pltpu.VMEM((tensors - 1, portion, rows_all), f32),
            pltpu.VMEM((rows_all, slots_dev * portion), bf16),
            pltpu.VMEM((CHUNKS, stores, group_rows, chunk), bf16),
            pltpu.VMEM((CHUNKS, 2, group_rows, chunk), bf16),
            pltpu.VMEM((CHUNKS, group_rows, chunk), bf16),
            pltpu.VMEM((CHUNKS, group_rows, chunk), bf16),
            pltpu.VMEM((CHUNKS, tensors, rows_dev, chunk), bf16),
            pltpu.VMEM((CHUNKS, tensors - 1, rows_dev, chunk), bf16),
            dma((2,)),
            dma((WEIGHT_SLOTS,)),
            dma((2, tensors)),
            dma((2, 3, tensors)),
            dma((2, 3)),
            dma((2, tensors)),
            dma((2, 2, CHUNKS)),
            dma((2, CHUNKS)),
            dma((2, tensors, CHUNKS)),
        ],
        compiler_params=pltpu.CompilerParams(
            collective_id=0, has_side_effects=True, vmem_limit_bytes=VMEM_BYTES
        ),
        cost_estimate=pl.CostEstimate(
            flops=2 * model * (group_rows * width + 2 * rows_all * slots_dev * portion),
            bytes_accessed=2 * (output_weight.size + shrink_matrices.size + expand_matrices.size),
            transcendentals=0,
        ),
    )(att, own_slots, hidden, output_weight, shrink_matrices, expand_matrices)


def attend(queries, cached_key_rows, cached_value_rows, cache_length):
    rows_dev, kv_heads, positions, head_dim = cached_key_rows.shape
    grouped = queries.reshape(rows_dev, kv_heads, -1, head_dim)
    scores = jnp.einsum(
        "rkgd,rkpd->rkgp", grouped, cached_key_rows, preferred_element_type=jnp.float32
    ) * head_dim ** (-0.5)
    live_pos = lax.broadcasted_iota(jnp.int32, (rows_dev, positions), 1) < cache_length[:, None]
    scores = jnp.where(live_pos[:, None, None, :], scores, -jnp.inf)
    highest = jnp.max(scores, axis=-1, keepdims=True)
    raised = jnp.exp(scores - highest)
    weights = (raised / jnp.sum(raised, axis=-1, keepdims=True)).astype(jnp.bfloat16)
    outputs = jnp.einsum(
        "rkgp,rkpd->rkgd", weights, cached_value_rows, preferred_element_type=jnp.float32
    )
    return outputs.astype(jnp.bfloat16).reshape(rows_dev, -1)


def place_in_owner(owner_ids, store_count):
    owner_hot = (owner_ids[..., None] == jnp.arange(store_count, dtype=jnp.int32)).astype(jnp.int32)
    return jnp.sum(jnp.cumsum(owner_hot, axis=-2) * owner_hot, axis=-1) - 1


def on_device(
    hidden,
    queries,
    cached_key_rows,
    cached_value_rows,
    cache_length,
    output_weight,
    shrink_matrices,
    expand_matrices,
    block_slot_rows,
    adapter_per_block,
    adapter_store_slot,
):
    attended = attend(queries, cached_key_rows, cached_value_rows, cache_length)
    head_rows = lax.all_to_all(attended, "tensor", split_axis=1, concat_axis=0, tiled=True)
    group_rows = head_rows.shape[0]
    slots_per_holder = shrink_matrices.shape[0]
    blocks_here = adapter_per_block.shape[0]
    capacity = blocks_here // 2
    store_count = lax.axis_size("store")
    rank_portion = expand_matrices.shape[1]
    slot_of = adapter_store_slot[adapter_per_block]
    requests = lax.all_gather(adapter_per_block, "store", axis=0, tiled=True)
    wanted = adapter_store_slot[requests].reshape(store_count, blocks_here)
    owner_all = wanted // slots_per_holder
    local_all = wanted % slots_per_holder
    position_all = place_in_owner(owner_all, store_count)
    store_index = lax.axis_index("store")
    chosen = (owner_all == store_index)[..., None] & (
        position_all[..., None] == jnp.arange(capacity, dtype=jnp.int32)
    )
    outgoing_local = jnp.sum(chosen.astype(jnp.int32) * local_all[..., None], axis=1)
    filled_rows = jnp.any(chosen, axis=1)
    empty_value = jnp.zeros((), jnp.bfloat16)
    outgoing_shrink = jnp.where(
        filled_rows[..., None, None], shrink_matrices[outgoing_local], empty_value
    )
    outgoing_expand = jnp.where(
        filled_rows[..., None, None], expand_matrices[outgoing_local], empty_value
    )
    recv_a, recv_b = (
        lax.all_to_all(outgoing_shrink, "store", split_axis=0, concat_axis=0, tiled=True),
        lax.all_to_all(outgoing_expand, "store", split_axis=0, concat_axis=0, tiled=True),
    )
    owner_mine = slot_of // slots_per_holder
    position_mine = place_in_owner(owner_mine, store_count)
    flat_place = owner_mine * capacity + position_mine
    fetched_a = recv_a.reshape((store_count * capacity,) + recv_a.shape[2:])[flat_place]
    fetched_b = recv_b.reshape((store_count * capacity,) + recv_b.shape[2:])[flat_place]
    live_slot = block_slot_rows >= 0
    picked = jnp.where(
        live_slot[..., None],
        head_rows[jnp.maximum(block_slot_rows, 0)],
        jnp.zeros((), jnp.bfloat16),
    )
    shrink_part = jnp.einsum("bsh,brh->bsr", picked, fetched_a, preferred_element_type=jnp.float32)
    summed_shrink = lax.psum(shrink_part, "tensor")
    shrink_output = lax.dynamic_slice_in_dim(
        summed_shrink, lax.axis_index("tensor") * rank_portion, rank_portion, 2
    )
    shrink_output = shrink_output.astype(jnp.bfloat16)
    targets = jnp.where(live_slot, block_slot_rows, group_rows)
    block_ids = lax.broadcasted_iota(jnp.int32, block_slot_rows.shape, 0)
    row_shrink = (
        jnp.zeros((group_rows + 1, blocks_here, rank_portion), jnp.bfloat16)
        .at[targets, block_ids]
        .set(shrink_output)
    )
    row_shrink = row_shrink[:group_rows].reshape(group_rows, blocks_here * rank_portion)
    stacked_b = fetched_b.reshape(blocks_here * rank_portion, -1)
    summed = lax.psum_scatter(
        jnp.dot(head_rows, output_weight, preferred_element_type=jnp.float32)
        + ADAPTER_SCALE * jnp.dot(row_shrink, stacked_b, preferred_element_type=jnp.float32),
        "tensor",
        scatter_dimension=0,
        tiled=True,
    )
    return (hidden.astype(jnp.float32) + summed).astype(jnp.bfloat16)


def solution(mesh):
    in_specs = (
        P(("groups", "store", "tensor"), None),
        P(("groups", "store", "tensor"), None),
        P(("groups", "store", "tensor"), None, None, None),
        P(("groups", "store", "tensor"), None, None, None),
        P(("groups", "store", "tensor")),
        P("tensor", None),
        P(("groups", "store"), None, "tensor"),
        P(("groups", "store"), "tensor", None),
        P(("groups", "store"), None),
        P(("groups", "store")),
        P("groups"),
    )
    out_specs = P(("groups", "store", "tensor"), None)
    tensors, stores = mesh.shape["tensor"], mesh.shape["store"]

    def plan(*args):
        rows_dev, model = args[0].shape
        fits = stores * tensors * rows_dev * model * 2 <= 4 * 1024 * 1024
        return (rows_plan if stores == 4 and rows_dev % 16 == 0 and fits else on_device)(*args)

    return jax.shard_map(
        plan, mesh=mesh, in_specs=in_specs, out_specs=out_specs, check_vma=False
    )
```

```python
import functools

import jax
import jax.numpy as jnp
from jax import lax
from jax.experimental import pallas as pl
from jax.experimental.pallas import tpu as pltpu
from jax.sharding import PartitionSpec as P

ADAPTER_SCALE = 2.0
MESH = pl.DeviceIdType.MESH
CHUNKS = 8
WEIGHT_SLOTS = 4
VMEM_BYTES = 60 * 1024 * 1024


def project_kernel(
    length_ref,
    adapter_ref,
    table_ref,
    listed_ref,
    hidden_ref,
    q_ref,
    key_hbm,
    value_hbm,
    weight_hbm,
    shrink_hbm,
    expand_hbm,
    out_ref,
    key_ref,
    value_ref,
    live_ref,
    heads_ref,
    att_ref,
    rows_ref,
    slots_ref,
    weight_ref,
    shrink_ref,
    expand_ref,
    base_ref,
    part_ref,
    part_recv,
    mix_ref,
    delta_ref,
    near_recv,
    far_send,
    far_recv,
    line_send,
    line_recv,
    load_sem,
    cache_sem,
    weight_sem,
    turn_sem,
    rows_sem,
    slots_sem,
    part_sem,
    near_sem,
    far_sem,
    line_sem,
):
    store = lax.axis_index("store")
    tensor = lax.axis_index("tensor")
    tensors = lax.axis_size("tensor")
    stores = lax.axis_size("store")
    near = store + 1 - 2 * (store % 2)
    far = (store + 2) % 4
    cross = (near + 2) % 4
    slots_dev, rank, width = shrink_ref.shape
    portion = expand_ref.shape[1]
    rows_dev = att_ref.shape[1]
    _, _, kv_heads, positions, head_dim = key_ref.shape
    heads = width // head_dim
    group_rows = tensors * rows_dev
    rows_all = stores * group_rows
    chunk = weight_ref.shape[2]

    def line(step):
        return lax.rem(tensor + step, tensors)

    barrier = pltpu.get_barrier_semaphore()
    for step in range(1, tensors):
        pl.semaphore_signal(barrier, inc=1, device_id={"tensor": line(step)}, device_id_type=MESH)
    for other in (near, far, cross):
        pl.semaphore_signal(barrier, inc=1, device_id={"store": other}, device_id_type=MESH)
    shrink_load = pltpu.make_async_copy(shrink_hbm, shrink_ref, load_sem.at[0])
    expand_load = pltpu.make_async_copy(expand_hbm, expand_ref, load_sem.at[1])

    def weight_load(j):
        return pltpu.make_async_copy(
            weight_hbm.at[:, pl.ds(pl.multiple_of(j * chunk, chunk), chunk)],
            weight_ref.at[lax.rem(j, WEIGHT_SLOTS)],
            weight_sem.at[lax.rem(j, WEIGHT_SLOTS)],
        )

    def cache_loads(i):
        heads_of = pl.ds(line(lax.rem(i + 1, tensors)) * kv_heads, kv_heads)
        return [
            pltpu.make_async_copy(key_hbm.at[:, heads_of], key_ref.at[i], cache_sem.at[0, i]),
            pltpu.make_async_copy(value_hbm.at[:, heads_of], value_ref.at[i], cache_sem.at[1, i]),
        ]

    for i in range(tensors):
        for copy in cache_loads(i):
            copy.start()
    for j in range(2):
        weight_load(j).start()
    shrink_load.start()
    for j in range(2, WEIGHT_SLOTS):
        weight_load(j).start()
    expand_load.start()

    blocks, block_slots = listed_ref.shape
    row_ids = lax.broadcasted_iota(jnp.int32, (blocks, rows_all), 1) - store * group_rows
    block_ids = lax.broadcasted_iota(jnp.int32, (blocks, rows_all), 0)
    block_slot = jnp.zeros((blocks, rows_all), jnp.int32)
    for b in range(blocks):
        block_slot = jnp.where(block_ids == b, table_ref[adapter_ref[b]], block_slot)
    own_slots = jnp.full((blocks, rows_all), -1, jnp.int32)
    for i in range(block_slots):
        named = (listed_ref[:, i : i + 1] == row_ids) & (row_ids >= 0)
        own_slots = jnp.where(named, block_slot, own_slots)
    slots_ref[store] = own_slots
    places = lax.broadcasted_iota(jnp.int32, live_ref.shape[1:], 1)
    for row in range(rows_dev):
        live_ref[row] = jnp.where(places < length_ref[row], 1, 0)
    pl.semaphore_wait(barrier, tensors - 1 + 3)

    def remote(src, dst, sems, at, **where):
        return pltpu.make_async_remote_copy(
            src_ref=src,
            dst_ref=dst,
            send_sem=sems.at[(0,) + at],
            recv_sem=sems.at[(1,) + at],
            device_id=where,
            device_id_type=MESH,
        )

    slot_copies = [
        remote(slots_ref.at[store], slots_ref.at[store], slots_sem, (i,), store=other)
        for i, other in enumerate((near, far, cross))
    ]
    for copy in slot_copies:
        copy.start()

    def turn(step):
        return remote(
            att_ref.at[line(step)], rows_ref.at[store, tensor], turn_sem, (step,), tensor=line(step)
        )

    def share(step):
        block = rows_ref.at[store, lax.rem(tensor + tensors - step, tensors)]
        return [
            remote(block, block, rows_sem, (0, step), store=far),
            remote(block, block, rows_sem, (1, step), store=near),
        ]

    def attend(i):
        target = line(lax.rem(i + 1, tensors))
        for head in range(heads):
            first = pl.multiple_of(target * width + head * head_dim, head_dim)
            heads_ref[pl.ds(head, rows_dev, stride=heads), :] = q_ref[
                :, pl.ds(first, head_dim)
            ].astype(jnp.float32)
        for copy in cache_loads(i):
            copy.wait()
        q = heads_ref[...].astype(jnp.bfloat16).reshape(rows_dev * kv_heads, -1, head_dim)
        scores = lax.dot_general(
            q,
            key_ref[i].reshape(rows_dev * kv_heads, positions, head_dim),
            (((2,), (2,)), ((0,), (0,))),
            preferred_element_type=jnp.float32,
        ) * head_dim ** (-0.5)
        live = (live_ref[...] > 0)[:, None]
        scores = scores.reshape((rows_dev, kv_heads) + scores.shape[1:])
        scores = jnp.where(live, scores, -jnp.inf)
        highest = jnp.max(scores, axis=-1, keepdims=True)
        raised = jnp.exp(scores - highest)
        weights = (raised / jnp.sum(raised, axis=-1, keepdims=True)).astype(jnp.bfloat16)
        outputs = lax.dot_general(
            weights.reshape(rows_dev * kv_heads, -1, positions),
            value_ref[i].reshape(rows_dev * kv_heads, positions, head_dim),
            (((2,), (1,)), ((0,), (0,))),
            preferred_element_type=jnp.float32,
        )
        heads_ref[...] = outputs.reshape(rows_dev * heads, head_dim)
        for head in range(heads):
            att_ref[target, :, head * head_dim : (head + 1) * head_dim] = heads_ref[
                pl.ds(head, rows_dev, stride=heads), :
            ].astype(jnp.bfloat16)

    def attend_step(i, _):
        attend(i)
        turn(i + 1).start()

        @pl.when(i > 0)
        def _():
            turn(i).wait_recv()
            for copy in share(i):
                copy.start()

        return 0

    lax.fori_loop(0, tensors - 1, attend_step, 0)
    attend(tensors - 1)
    rows_ref[store, tensor] = att_ref[tensor]
    for copy in share(0):
        copy.start()
    turn(tensors - 1).wait_recv()
    for copy in share(tensors - 1):
        copy.start()
    turns = [turn(step) for step in range(1, tensors)]
    shares = [share(step) for step in range(tensors)]

    own_rows = rows_ref.at[store]

    def project(j, _):
        weight_load(j).wait()
        base_ref[j] = jnp.dot(
            own_rows[...].reshape(group_rows, width),
            weight_ref[lax.rem(j, WEIGHT_SLOTS)],
            preferred_element_type=jnp.float32,
        )
        return 0

    relays = []
    for step in range(tensors):
        block = rows_ref.at[far, lax.rem(tensor + tensors - step, tensors)]
        relays.append(remote(block, block, rows_sem, (2, step), store=near))

    lax.fori_loop(0, 2, project, 0)
    for step in range(tensors):
        shares[step][0].wait_recv()
        relays[step].start()
    lax.fori_loop(2, WEIGHT_SLOTS, project, 0)
    for j in range(WEIGHT_SLOTS, min(2 * WEIGHT_SLOTS, CHUNKS)):
        weight_load(j).start()
    for copy in slot_copies:
        copy.wait_recv()
    for step in range(tensors):
        shares[step][1].wait_recv()
        relays[step].wait_recv()
    shrink_load.wait()

    slot_row = jnp.max(jnp.max(slots_ref[...], axis=0), axis=0, keepdims=True) - store * slots_dev
    batch = 4
    part_ref[...] = jnp.zeros_like(part_ref)

    def shrink_step(i, _):
        first = i * batch
        product = lax.dot_general(
            shrink_ref[pl.ds(first, batch)].reshape(batch * rank, width),
            rows_ref[...].reshape(rows_all, width),
            (((1,), (1,)), ((), ())),
            preferred_element_type=jnp.float32,
        ).reshape(batch, rank, rows_all)
        total = jnp.zeros((rank, rows_all), jnp.float32)
        for b in range(batch):
            total += jnp.where(slot_row == first + b, product[b], 0.0)
        part_ref[...] += total.reshape(part_ref.shape)
        return 0

    lax.fori_loop(0, slots_dev // batch, shrink_step, 0)
    parts = [
        remote(part_ref.at[line(step)], part_recv.at[step - 1], part_sem, (step,), tensor=line(step))
        for step in range(1, tensors)
    ]
    for copy in parts:
        copy.start()
    lax.fori_loop(WEIGHT_SLOTS, CHUNKS - 2, project, 0)
    shrunk = part_ref[tensor]
    for step in range(1, tensors):
        parts[step - 1].wait_recv()
        shrunk += part_recv[step - 1]
    shrunk = ADAPTER_SCALE * shrunk.astype(jnp.bfloat16).astype(jnp.float32)
    slot_ids = lax.broadcasted_iota(jnp.int32, (slots_dev, portion, rows_all), 0)
    spread = jnp.where(slot_row[None] == slot_ids, shrunk[None], 0.0)
    mix_ref[...] = spread.reshape(slots_dev * portion, rows_all).T.astype(jnp.bfloat16)
    expand_load.wait()

    def near_copies(j):
        return [
            remote(delta_ref.at[j, near], near_recv.at[j, 0], near_sem, (0, j), store=near),
            remote(delta_ref.at[j, cross], near_recv.at[j, 1], near_sem, (1, j), store=near),
        ]

    def far_copy(j):
        return remote(far_send.at[j], far_recv.at[j], far_sem, (j,), store=far)

    def line_copies(j):
        return [
            remote(
                line_send.at[j, line(step)], line_recv.at[j, step - 1], line_sem, (step, j), tensor=line(step)
            )
            for step in range(1, tensors)
        ]

    def columns(j):
        return pl.ds(pl.multiple_of(j * chunk, chunk), chunk)

    def send_far(j):
        near_copies(j)[1].wait_recv()
        total = delta_ref[j, far].astype(jnp.float32) + near_recv[j, 1].astype(jnp.float32)
        far_send[j] = total.astype(jnp.bfloat16)
        far_copy(j).start()

    def expand_step(j, _):
        delta_ref[j] = (
            jnp.dot(
                mix_ref[...],
                expand_ref[:, :, columns(j)].reshape(slots_dev * portion, chunk),
                preferred_element_type=jnp.float32,
            )
            .astype(jnp.bfloat16)
            .reshape(stores, group_rows, chunk)
        )
        for copy in reversed(near_copies(j)):
            copy.start()

        @pl.when(j > 0)
        def _():
            send_far(j - 1)

        return 0

    lax.fori_loop(0, CHUNKS, expand_step, 0)
    send_far(CHUNKS - 1)
    lax.fori_loop(CHUNKS - 2, CHUNKS, project, 0)

    def line_step(j, _):
        near_copies(j)[0].wait_recv()
        far_copy(j).wait_recv()
        total = (
            base_ref[j]
            + delta_ref[j, store].astype(jnp.float32)
            + near_recv[j, 0].astype(jnp.float32)
            + far_recv[j].astype(jnp.float32)
        )
        line_send[j] = total.astype(jnp.bfloat16).reshape(tensors, rows_dev, chunk)
        for copy in line_copies(j):
            copy.start()
        return 0

    lax.fori_loop(0, CHUNKS, line_step, 0)

    def last_step(j, _):
        total = hidden_ref[:, columns(j)].astype(jnp.float32) + line_send[j, tensor].astype(jnp.float32)
        for step, copy in enumerate(line_copies(j)):
            copy.wait_recv()
            total += line_recv[j, step].astype(jnp.float32)
        out_ref[:, columns(j)] = total.astype(jnp.bfloat16)
        return 0

    lax.fori_loop(0, CHUNKS, last_step, 0)

    for copy in turns + slot_copies + relays + parts:
        copy.wait_send()
    for pair in shares:
        for copy in pair:
            copy.wait_send()

    def drain(j, _):
        for copy in near_copies(j) + [far_copy(j)] + line_copies(j):
            copy.wait_send()
        return 0

    lax.fori_loop(0, CHUNKS, drain, 0)


def rows_plan(
    hidden,
    queries,
    cached_key_rows,
    cached_value_rows,
    cache_length,
    output_weight,
    shrink_matrices,
    expand_matrices,
    block_slot_rows,
    adapter_per_block,
    adapter_store_slot,
):
    tensors = lax.axis_size("tensor")
    stores = lax.axis_size("store")
    rows_dev, model = hidden.shape
    width = output_weight.shape[0]
    slots_dev, rank, _ = shrink_matrices.shape
    portion = expand_matrices.shape[1]
    group_rows = tensors * rows_dev
    rows_all = stores * group_rows
    chunk = model // CHUNKS

    kv_heads, positions, head_dim = cached_key_rows.shape[1:]
    heads = width // head_dim
    kv_part = kv_heads // tensors

    vmem = pl.BlockSpec(memory_space=pltpu.VMEM)
    smem = pl.BlockSpec(memory_space=pltpu.SMEM)
    hbm = pl.BlockSpec(memory_space=pl.ANY)
    bf16, f32 = jnp.bfloat16, jnp.float32
    dma = pltpu.SemaphoreType.DMA
    return pl.pallas_call(
        project_kernel,
        out_shape=jax.ShapeDtypeStruct((rows_dev, model), bf16),
        in_specs=[smem, smem, smem, vmem, vmem, vmem, hbm, hbm, hbm, hbm, hbm],
        out_specs=vmem,
        scratch_shapes=[
            pltpu.VMEM((tensors, rows_dev, kv_part, positions, head_dim), bf16),
            pltpu.VMEM((tensors, rows_dev, kv_part, positions, head_dim), bf16),
            pltpu.VMEM((rows_dev, heads // kv_part, positions), jnp.int32),
            pltpu.VMEM((rows_dev * heads, head_dim), f32),
            pltpu.VMEM((tensors, rows_dev, width), bf16),
            pltpu.VMEM((stores, tensors, rows_dev, width), bf16),
            pltpu.VMEM((stores, 8, rows_all), jnp.int32),
            pltpu.VMEM((WEIGHT_SLOTS, width, chunk), bf16),
            pltpu.VMEM((slots_dev, rank, width), bf16),
            pltpu.VMEM((slots_dev, portion, model), bf16),
            pltpu.VMEM((CHUNKS, group_rows, chunk), f32),
            pltpu.VMEM((tensors, portion, rows_all), f32),
            pltpu.VMEM((tensors - 1, portion, rows_all), f32),
            pltpu.VMEM((rows_all, slots_dev * portion), bf16),
            pltpu.VMEM((CHUNKS, stores, group_rows, chunk), bf16),
            pltpu.VMEM((CHUNKS, 2, group_rows, chunk), bf16),
            pltpu.VMEM((CHUNKS, group_rows, chunk), bf16),
            pltpu.VMEM((CHUNKS, group_rows, chunk), bf16),
            pltpu.VMEM((CHUNKS, tensors, rows_dev, chunk), bf16),
            pltpu.VMEM((CHUNKS, tensors - 1, rows_dev, chunk), bf16),
            dma((2,)),
            dma((2, tensors)),
            dma((WEIGHT_SLOTS,)),
            dma((2, tensors)),
            dma((2, 3, tensors)),
            dma((2, 3)),
            dma((2, tensors)),
            dma((2, 2, CHUNKS)),
            dma((2, CHUNKS)),
            dma((2, tensors, CHUNKS)),
        ],
        compiler_params=pltpu.CompilerParams(
            collective_id=0, has_side_effects=True, vmem_limit_bytes=VMEM_BYTES
        ),
        cost_estimate=pl.CostEstimate(
            flops=2 * model * (group_rows * width + 2 * rows_all * slots_dev * portion),
            bytes_accessed=2 * (output_weight.size + shrink_matrices.size + expand_matrices.size),
            transcendentals=0,
        ),
    )(
        cache_length,
        adapter_per_block,
        adapter_store_slot,
        block_slot_rows,
        hidden,
        queries,
        cached_key_rows,
        cached_value_rows,
        output_weight,
        shrink_matrices,
        expand_matrices,
    )


def attend(queries, cached_key_rows, cached_value_rows, cache_length):
    rows_dev, kv_heads, positions, head_dim = cached_key_rows.shape
    grouped = queries.reshape(rows_dev, kv_heads, -1, head_dim)
    scores = jnp.einsum(
        "rkgd,rkpd->rkgp", grouped, cached_key_rows, preferred_element_type=jnp.float32
    ) * head_dim ** (-0.5)
    live_pos = lax.broadcasted_iota(jnp.int32, (rows_dev, positions), 1) < cache_length[:, None]
    scores = jnp.where(live_pos[:, None, None, :], scores, -jnp.inf)
    highest = jnp.max(scores, axis=-1, keepdims=True)
    raised = jnp.exp(scores - highest)
    weights = (raised / jnp.sum(raised, axis=-1, keepdims=True)).astype(jnp.bfloat16)
    outputs = jnp.einsum(
        "rkgp,rkpd->rkgd", weights, cached_value_rows, preferred_element_type=jnp.float32
    )
    return outputs.astype(jnp.bfloat16).reshape(rows_dev, -1)


def place_in_owner(owner_ids, store_count):
    owner_hot = (owner_ids[..., None] == jnp.arange(store_count, dtype=jnp.int32)).astype(jnp.int32)
    return jnp.sum(jnp.cumsum(owner_hot, axis=-2) * owner_hot, axis=-1) - 1


def on_device(
    hidden,
    queries,
    cached_key_rows,
    cached_value_rows,
    cache_length,
    output_weight,
    shrink_matrices,
    expand_matrices,
    block_slot_rows,
    adapter_per_block,
    adapter_store_slot,
):
    attended = attend(queries, cached_key_rows, cached_value_rows, cache_length)
    head_rows = lax.all_to_all(attended, "tensor", split_axis=1, concat_axis=0, tiled=True)
    group_rows = head_rows.shape[0]
    slots_per_holder = shrink_matrices.shape[0]
    blocks_here = adapter_per_block.shape[0]
    capacity = blocks_here // 2
    store_count = lax.axis_size("store")
    rank_portion = expand_matrices.shape[1]
    slot_of = adapter_store_slot[adapter_per_block]
    requests = lax.all_gather(adapter_per_block, "store", axis=0, tiled=True)
    wanted = adapter_store_slot[requests].reshape(store_count, blocks_here)
    owner_all = wanted // slots_per_holder
    local_all = wanted % slots_per_holder
    position_all = place_in_owner(owner_all, store_count)
    store_index = lax.axis_index("store")
    chosen = (owner_all == store_index)[..., None] & (
        position_all[..., None] == jnp.arange(capacity, dtype=jnp.int32)
    )
    outgoing_local = jnp.sum(chosen.astype(jnp.int32) * local_all[..., None], axis=1)
    filled_rows = jnp.any(chosen, axis=1)
    empty_value = jnp.zeros((), jnp.bfloat16)
    outgoing_shrink = jnp.where(
        filled_rows[..., None, None], shrink_matrices[outgoing_local], empty_value
    )
    outgoing_expand = jnp.where(
        filled_rows[..., None, None], expand_matrices[outgoing_local], empty_value
    )
    recv_a, recv_b = (
        lax.all_to_all(outgoing_shrink, "store", split_axis=0, concat_axis=0, tiled=True),
        lax.all_to_all(outgoing_expand, "store", split_axis=0, concat_axis=0, tiled=True),
    )
    owner_mine = slot_of // slots_per_holder
    position_mine = place_in_owner(owner_mine, store_count)
    flat_place = owner_mine * capacity + position_mine
    fetched_a = recv_a.reshape((store_count * capacity,) + recv_a.shape[2:])[flat_place]
    fetched_b = recv_b.reshape((store_count * capacity,) + recv_b.shape[2:])[flat_place]
    live_slot = block_slot_rows >= 0
    picked = jnp.where(
        live_slot[..., None],
        head_rows[jnp.maximum(block_slot_rows, 0)],
        jnp.zeros((), jnp.bfloat16),
    )
    shrink_part = jnp.einsum("bsh,brh->bsr", picked, fetched_a, preferred_element_type=jnp.float32)
    summed_shrink = lax.psum(shrink_part, "tensor")
    shrink_output = lax.dynamic_slice_in_dim(
        summed_shrink, lax.axis_index("tensor") * rank_portion, rank_portion, 2
    )
    shrink_output = shrink_output.astype(jnp.bfloat16)
    targets = jnp.where(live_slot, block_slot_rows, group_rows)
    block_ids = lax.broadcasted_iota(jnp.int32, block_slot_rows.shape, 0)
    row_shrink = (
        jnp.zeros((group_rows + 1, blocks_here, rank_portion), jnp.bfloat16)
        .at[targets, block_ids]
        .set(shrink_output)
    )
    row_shrink = row_shrink[:group_rows].reshape(group_rows, blocks_here * rank_portion)
    stacked_b = fetched_b.reshape(blocks_here * rank_portion, -1)
    summed = lax.psum_scatter(
        jnp.dot(head_rows, output_weight, preferred_element_type=jnp.float32)
        + ADAPTER_SCALE * jnp.dot(row_shrink, stacked_b, preferred_element_type=jnp.float32),
        "tensor",
        scatter_dimension=0,
        tiled=True,
    )
    return (hidden.astype(jnp.float32) + summed).astype(jnp.bfloat16)


def solution(mesh):
    in_specs = (
        P(("groups", "store", "tensor"), None),
        P(("groups", "store", "tensor"), None),
        P(("groups", "store", "tensor"), None, None, None),
        P(("groups", "store", "tensor"), None, None, None),
        P(("groups", "store", "tensor")),
        P("tensor", None),
        P(("groups", "store"), None, "tensor"),
        P(("groups", "store"), "tensor", None),
        P(("groups", "store"), None),
        P(("groups", "store")),
        P("groups"),
    )
    out_specs = P(("groups", "store", "tensor"), None)
    tensors, stores = mesh.shape["tensor"], mesh.shape["store"]

    def plan(*args):
        rows_dev, model = args[0].shape
        kv_heads = args[2].shape[1]
        fits = stores * tensors * rows_dev * model * 2 <= 4 * 1024 * 1024
        fits = fits and stores == 4 and rows_dev % 16 == 0 and kv_heads % tensors == 0
        return (rows_plan if fits else on_device)(*args)

    return jax.shard_map(
        plan, mesh=mesh, in_specs=in_specs, out_specs=out_specs, check_vma=False
    )
```

```python
import functools

import jax
import jax.numpy as jnp
from jax import lax
from jax.experimental import pallas as pl
from jax.experimental.pallas import tpu as pltpu
from jax.sharding import PartitionSpec as P

ADAPTER_SCALE = 2.0
MESH = pl.DeviceIdType.MESH
CHUNKS = 8
WEIGHT_SLOTS = 4
FIRST = 4
EARLY = 8
VMEM_BYTES = 60 * 1024 * 1024


def project_kernel(
    length_ref,
    adapter_ref,
    table_ref,
    listed_ref,
    hidden_ref,
    q_ref,
    key_hbm,
    value_hbm,
    weight_hbm,
    shrink_hbm,
    expand_hbm,
    out_ref,
    key_ref,
    value_ref,
    live_ref,
    heads_ref,
    att_ref,
    rows_ref,
    slots_ref,
    weight_ref,
    shrink_ref,
    expand_ref,
    base_ref,
    part_ref,
    part_recv,
    mix_ref,
    delta_ref,
    near_recv,
    far_send,
    far_recv,
    line_send,
    line_recv,
    load_sem,
    cache_sem,
    weight_sem,
    turn_sem,
    rows_sem,
    slots_sem,
    part_sem,
    near_sem,
    far_sem,
    line_sem,
):
    store = lax.axis_index("store")
    tensor = lax.axis_index("tensor")
    tensors = lax.axis_size("tensor")
    stores = lax.axis_size("store")
    near = store + 1 - 2 * (store % 2)
    far = (store + 2) % 4
    cross = (near + 2) % 4
    slots_dev, rank, width = shrink_ref.shape
    portion = expand_ref.shape[1]
    rows_dev = att_ref.shape[1]
    _, _, kv_heads, positions, head_dim = key_ref.shape
    heads = width // head_dim
    group_rows = tensors * rows_dev
    rows_all = stores * group_rows
    chunk = weight_ref.shape[2]

    def line(step):
        return lax.rem(tensor + step, tensors)

    barrier = pltpu.get_barrier_semaphore()
    for step in range(1, tensors):
        pl.semaphore_signal(barrier, inc=1, device_id={"tensor": line(step)}, device_id_type=MESH)
    for other in (near, far, cross):
        pl.semaphore_signal(barrier, inc=1, device_id={"store": other}, device_id_type=MESH)
    shrink_load = pltpu.make_async_copy(shrink_hbm, shrink_ref, load_sem.at[0])
    expand_load = pltpu.make_async_copy(expand_hbm, expand_ref, load_sem.at[1])

    def weight_load(j):
        return pltpu.make_async_copy(
            weight_hbm.at[:, pl.ds(pl.multiple_of(j * chunk, chunk), chunk)],
            weight_ref.at[lax.rem(j, WEIGHT_SLOTS)],
            weight_sem.at[lax.rem(j, WEIGHT_SLOTS)],
        )

    def cache_loads(i):
        heads_of = pl.ds(line(i) * kv_heads, kv_heads)
        return [
            pltpu.make_async_copy(key_hbm.at[:, heads_of], key_ref.at[i], cache_sem.at[0, i]),
            pltpu.make_async_copy(value_hbm.at[:, heads_of], value_ref.at[i], cache_sem.at[1, i]),
        ]

    for i in range(tensors):
        for copy in cache_loads(i):
            copy.start()
    blocks, block_slots = listed_ref.shape
    row_ids = lax.broadcasted_iota(jnp.int32, (blocks, rows_all), 1) - store * group_rows
    block_ids = lax.broadcasted_iota(jnp.int32, (blocks, rows_all), 0)
    block_slot = jnp.zeros((blocks, rows_all), jnp.int32)
    for b in range(blocks):
        block_slot = jnp.where(block_ids == b, table_ref[adapter_ref[b]], block_slot)
    own_slots = jnp.full((blocks, rows_all), -1, jnp.int32)
    for i in range(block_slots):
        named = (listed_ref[:, i : i + 1] == row_ids) & (row_ids >= 0)
        own_slots = jnp.where(named, block_slot, own_slots)
    slots_ref[store] = own_slots
    places = lax.broadcasted_iota(jnp.int32, live_ref.shape[1:], 1)
    for row in range(rows_dev):
        live_ref[row] = jnp.where(places < length_ref[row], 1, 0)

    def remote(src, dst, sems, at, **where):
        return pltpu.make_async_remote_copy(
            src_ref=src,
            dst_ref=dst,
            send_sem=sems.at[(0,) + at],
            recv_sem=sems.at[(1,) + at],
            device_id=where,
            device_id_type=MESH,
        )

    def turn(step):
        return remote(
            att_ref.at[line(step)], rows_ref.at[store, tensor], turn_sem, (step,), tensor=line(step)
        )

    def share(step):
        block = rows_ref.at[store, lax.rem(tensor + tensors - step, tensors)]
        return [
            remote(block, block, rows_sem, (0, step), store=far),
            remote(block, block, rows_sem, (1, step), store=near),
        ]

    def follow(i):
        @pl.when(i == 0)
        def _():
            shrink_load.start()

        @pl.when(i == 1)
        def _():
            expand_load.start()

        @pl.when(i == 2)
        def _():
            for j in range(WEIGHT_SLOTS):
                weight_load(j).start()

    def attend(i):
        target = line(i)
        for head in range(heads):
            first = pl.multiple_of(target * width + head * head_dim, head_dim)
            heads_ref[pl.ds(head, rows_dev, stride=heads), :] = q_ref[
                :, pl.ds(first, head_dim)
            ].astype(jnp.float32)
        for copy in cache_loads(i):
            copy.wait()
        follow(i)
        q = heads_ref[...].astype(jnp.bfloat16).reshape(rows_dev * kv_heads, -1, head_dim)
        scores = lax.dot_general(
            q,
            key_ref[i].reshape(rows_dev * kv_heads, positions, head_dim),
            (((2,), (2,)), ((0,), (0,))),
            preferred_element_type=jnp.float32,
        ) * head_dim ** (-0.5)
        live = (live_ref[...] > 0)[:, None]
        scores = scores.reshape((rows_dev, kv_heads) + scores.shape[1:])
        scores = jnp.where(live, scores, -jnp.inf)
        highest = jnp.max(scores, axis=-1, keepdims=True)
        raised = jnp.exp(scores - highest)
        weights = (raised / jnp.sum(raised, axis=-1, keepdims=True)).astype(jnp.bfloat16)
        outputs = lax.dot_general(
            weights.reshape(rows_dev * kv_heads, -1, positions),
            value_ref[i].reshape(rows_dev * kv_heads, positions, head_dim),
            (((2,), (1,)), ((0,), (0,))),
            preferred_element_type=jnp.float32,
        )
        heads_ref[...] = outputs.reshape(rows_dev * heads, head_dim)
        for head in range(heads):
            att_ref[target, :, head * head_dim : (head + 1) * head_dim] = heads_ref[
                pl.ds(head, rows_dev, stride=heads), :
            ].astype(jnp.bfloat16)

    def attend_step(i, _):
        attend(i)
        turn(i).start()

        @pl.when(i > 1)
        def _():
            turn(i - 1).wait_recv()
            for copy in share(i - 1):
                copy.start()

        return 0

    attend(0)
    rows_ref[store, tensor] = att_ref[tensor]
    pl.semaphore_wait(barrier, tensors - 1 + 3)
    for copy in share(0):
        copy.start()
    lax.fori_loop(1, tensors, attend_step, 0)
    turn(tensors - 1).wait_recv()
    for copy in share(tensors - 1):
        copy.start()
    slot_copies = [
        remote(slots_ref.at[store], slots_ref.at[store], slots_sem, (i,), store=other)
        for i, other in enumerate((near, far, cross))
    ]
    for copy in slot_copies:
        copy.start()
    turns = [turn(step) for step in range(1, tensors)]
    shares = [share(step) for step in range(tensors)]

    own_rows = rows_ref.at[store]

    def project(j, _):
        weight_load(j).wait()
        base_ref[j] = jnp.dot(
            own_rows[...].reshape(group_rows, width),
            weight_ref[lax.rem(j, WEIGHT_SLOTS)],
            preferred_element_type=jnp.float32,
        )

        @pl.when(j + WEIGHT_SLOTS < CHUNKS)
        def _():
            weight_load(j + WEIGHT_SLOTS).start()

        return 0

    relays = []
    for step in range(tensors):
        block = rows_ref.at[far, lax.rem(tensor + tensors - step, tensors)]
        relays.append(remote(block, block, rows_sem, (2, step), store=near))

    lax.fori_loop(0, FIRST, project, 0)
    for step in range(tensors):
        shares[step][0].wait_recv()
        relays[step].start()
    for copy in slot_copies:
        copy.wait_recv()
    for step in range(tensors):
        shares[step][1].wait_recv()
        relays[step].wait_recv()
    shrink_load.wait()

    slot_row = jnp.max(jnp.max(slots_ref[...], axis=0), axis=0, keepdims=True) - store * slots_dev
    batch = 4
    part_ref[...] = jnp.zeros_like(part_ref)

    def shrink_step(i, _):
        first = i * batch
        product = lax.dot_general(
            shrink_ref[pl.ds(first, batch)].reshape(batch * rank, width),
            rows_ref[...].reshape(rows_all, width),
            (((1,), (1,)), ((), ())),
            preferred_element_type=jnp.float32,
        ).reshape(batch, rank, rows_all)
        total = jnp.zeros((rank, rows_all), jnp.float32)
        for b in range(batch):
            total += jnp.where(slot_row == first + b, product[b], 0.0)
        part_ref[...] += total.reshape(part_ref.shape)
        return 0

    lax.fori_loop(0, slots_dev // batch, shrink_step, 0)
    parts = [
        remote(part_ref.at[line(step)], part_recv.at[step - 1], part_sem, (step,), tensor=line(step))
        for step in range(1, tensors)
    ]
    for copy in parts:
        copy.start()
    lax.fori_loop(FIRST, EARLY, project, 0)
    shrunk = part_ref[tensor]
    for step in range(1, tensors):
        parts[step - 1].wait_recv()
        shrunk += part_recv[step - 1]
    shrunk = ADAPTER_SCALE * shrunk.astype(jnp.bfloat16).astype(jnp.float32)
    slot_ids = lax.broadcasted_iota(jnp.int32, (slots_dev, portion, rows_all), 0)
    spread = jnp.where(slot_row[None] == slot_ids, shrunk[None], 0.0)
    mix_ref[...] = spread.reshape(slots_dev * portion, rows_all).T.astype(jnp.bfloat16)
    expand_load.wait()

    def near_copies(j):
        return [
            remote(delta_ref.at[j, near], near_recv.at[j, 0], near_sem, (0, j), store=near),
            remote(delta_ref.at[j, cross], near_recv.at[j, 1], near_sem, (1, j), store=near),
        ]

    def far_copy(j):
        return remote(far_send.at[j], far_recv.at[j], far_sem, (j,), store=far)

    def line_copies(j):
        return [
            remote(
                line_send.at[j, line(step)], line_recv.at[j, step - 1], line_sem, (step, j), tensor=line(step)
            )
            for step in range(1, tensors)
        ]

    def columns(j):
        return pl.ds(pl.multiple_of(j * chunk, chunk), chunk)

    def send_far(j):
        near_copies(j)[1].wait_recv()
        total = delta_ref[j, far].astype(jnp.float32) + near_recv[j, 1].astype(jnp.float32)
        far_send[j] = total.astype(jnp.bfloat16)
        far_copy(j).start()

    def expand_step(j, _):
        delta_ref[j] = (
            jnp.dot(
                mix_ref[...],
                expand_ref[:, :, columns(j)].reshape(slots_dev * portion, chunk),
                preferred_element_type=jnp.float32,
            )
            .astype(jnp.bfloat16)
            .reshape(stores, group_rows, chunk)
        )
        for copy in reversed(near_copies(j)):
            copy.start()

        @pl.when(j > 0)
        def _():
            send_far(j - 1)

        return 0

    lax.fori_loop(0, CHUNKS, expand_step, 0)
    send_far(CHUNKS - 1)

    def line_step(j, _):
        near_copies(j)[0].wait_recv()
        far_copy(j).wait_recv()
        total = (
            base_ref[j]
            + delta_ref[j, store].astype(jnp.float32)
            + near_recv[j, 0].astype(jnp.float32)
            + far_recv[j].astype(jnp.float32)
        )
        line_send[j] = total.astype(jnp.bfloat16).reshape(tensors, rows_dev, chunk)
        for copy in line_copies(j):
            copy.start()
        return 0

    lax.fori_loop(0, CHUNKS, line_step, 0)

    def last_step(j, _):
        total = hidden_ref[:, columns(j)].astype(jnp.float32) + line_send[j, tensor].astype(jnp.float32)
        for step, copy in enumerate(line_copies(j)):
            copy.wait_recv()
            total += line_recv[j, step].astype(jnp.float32)
        out_ref[:, columns(j)] = total.astype(jnp.bfloat16)
        return 0

    lax.fori_loop(0, CHUNKS, last_step, 0)

    for copy in turns + slot_copies + relays + parts:
        copy.wait_send()
    for pair in shares:
        for copy in pair:
            copy.wait_send()

    def drain(j, _):
        for copy in near_copies(j) + [far_copy(j)] + line_copies(j):
            copy.wait_send()
        return 0

    lax.fori_loop(0, CHUNKS, drain, 0)


def rows_plan(
    hidden,
    queries,
    cached_key_rows,
    cached_value_rows,
    cache_length,
    output_weight,
    shrink_matrices,
    expand_matrices,
    block_slot_rows,
    adapter_per_block,
    adapter_store_slot,
):
    tensors = lax.axis_size("tensor")
    stores = lax.axis_size("store")
    rows_dev, model = hidden.shape
    width = output_weight.shape[0]
    slots_dev, rank, _ = shrink_matrices.shape
    portion = expand_matrices.shape[1]
    group_rows = tensors * rows_dev
    rows_all = stores * group_rows
    chunk = model // CHUNKS

    kv_heads, positions, head_dim = cached_key_rows.shape[1:]
    heads = width // head_dim
    kv_part = kv_heads // tensors

    vmem = pl.BlockSpec(memory_space=pltpu.VMEM)
    smem = pl.BlockSpec(memory_space=pltpu.SMEM)
    hbm = pl.BlockSpec(memory_space=pl.ANY)
    bf16, f32 = jnp.bfloat16, jnp.float32
    dma = pltpu.SemaphoreType.DMA
    return pl.pallas_call(
        project_kernel,
        out_shape=jax.ShapeDtypeStruct((rows_dev, model), bf16),
        in_specs=[smem, smem, smem, vmem, vmem, vmem, hbm, hbm, hbm, hbm, hbm],
        out_specs=vmem,
        scratch_shapes=[
            pltpu.VMEM((tensors, rows_dev, kv_part, positions, head_dim), bf16),
            pltpu.VMEM((tensors, rows_dev, kv_part, positions, head_dim), bf16),
            pltpu.VMEM((rows_dev, heads // kv_part, positions), jnp.int32),
            pltpu.VMEM((rows_dev * heads, head_dim), f32),
            pltpu.VMEM((tensors, rows_dev, width), bf16),
            pltpu.VMEM((stores, tensors, rows_dev, width), bf16),
            pltpu.VMEM((stores, 8, rows_all), jnp.int32),
            pltpu.VMEM((WEIGHT_SLOTS, width, chunk), bf16),
            pltpu.VMEM((slots_dev, rank, width), bf16),
            pltpu.VMEM((slots_dev, portion, model), bf16),
            pltpu.VMEM((CHUNKS, group_rows, chunk), f32),
            pltpu.VMEM((tensors, portion, rows_all), f32),
            pltpu.VMEM((tensors - 1, portion, rows_all), f32),
            pltpu.VMEM((rows_all, slots_dev * portion), bf16),
            pltpu.VMEM((CHUNKS, stores, group_rows, chunk), bf16),
            pltpu.VMEM((CHUNKS, 2, group_rows, chunk), bf16),
            pltpu.VMEM((CHUNKS, group_rows, chunk), bf16),
            pltpu.VMEM((CHUNKS, group_rows, chunk), bf16),
            pltpu.VMEM((CHUNKS, tensors, rows_dev, chunk), bf16),
            pltpu.VMEM((CHUNKS, tensors - 1, rows_dev, chunk), bf16),
            dma((2,)),
            dma((2, tensors)),
            dma((WEIGHT_SLOTS,)),
            dma((2, tensors)),
            dma((2, 3, tensors)),
            dma((2, 3)),
            dma((2, tensors)),
            dma((2, 2, CHUNKS)),
            dma((2, CHUNKS)),
            dma((2, tensors, CHUNKS)),
        ],
        compiler_params=pltpu.CompilerParams(
            collective_id=0, has_side_effects=True, vmem_limit_bytes=VMEM_BYTES
        ),
        cost_estimate=pl.CostEstimate(
            flops=2 * model * (group_rows * width + 2 * rows_all * slots_dev * portion),
            bytes_accessed=2 * (output_weight.size + shrink_matrices.size + expand_matrices.size),
            transcendentals=0,
        ),
    )(
        cache_length,
        adapter_per_block,
        adapter_store_slot,
        block_slot_rows,
        hidden,
        queries,
        cached_key_rows,
        cached_value_rows,
        output_weight,
        shrink_matrices,
        expand_matrices,
    )


def attend(queries, cached_key_rows, cached_value_rows, cache_length):
    rows_dev, kv_heads, positions, head_dim = cached_key_rows.shape
    grouped = queries.reshape(rows_dev, kv_heads, -1, head_dim)
    scores = jnp.einsum(
        "rkgd,rkpd->rkgp", grouped, cached_key_rows, preferred_element_type=jnp.float32
    ) * head_dim ** (-0.5)
    live_pos = lax.broadcasted_iota(jnp.int32, (rows_dev, positions), 1) < cache_length[:, None]
    scores = jnp.where(live_pos[:, None, None, :], scores, -jnp.inf)
    highest = jnp.max(scores, axis=-1, keepdims=True)
    raised = jnp.exp(scores - highest)
    weights = (raised / jnp.sum(raised, axis=-1, keepdims=True)).astype(jnp.bfloat16)
    outputs = jnp.einsum(
        "rkgp,rkpd->rkgd", weights, cached_value_rows, preferred_element_type=jnp.float32
    )
    return outputs.astype(jnp.bfloat16).reshape(rows_dev, -1)


def place_in_owner(owner_ids, store_count):
    owner_hot = (owner_ids[..., None] == jnp.arange(store_count, dtype=jnp.int32)).astype(jnp.int32)
    return jnp.sum(jnp.cumsum(owner_hot, axis=-2) * owner_hot, axis=-1) - 1


def on_device(
    hidden,
    queries,
    cached_key_rows,
    cached_value_rows,
    cache_length,
    output_weight,
    shrink_matrices,
    expand_matrices,
    block_slot_rows,
    adapter_per_block,
    adapter_store_slot,
):
    attended = attend(queries, cached_key_rows, cached_value_rows, cache_length)
    head_rows = lax.all_to_all(attended, "tensor", split_axis=1, concat_axis=0, tiled=True)
    group_rows = head_rows.shape[0]
    slots_per_holder = shrink_matrices.shape[0]
    blocks_here = adapter_per_block.shape[0]
    capacity = blocks_here // 2
    store_count = lax.axis_size("store")
    rank_portion = expand_matrices.shape[1]
    slot_of = adapter_store_slot[adapter_per_block]
    requests = lax.all_gather(adapter_per_block, "store", axis=0, tiled=True)
    wanted = adapter_store_slot[requests].reshape(store_count, blocks_here)
    owner_all = wanted // slots_per_holder
    local_all = wanted % slots_per_holder
    position_all = place_in_owner(owner_all, store_count)
    store_index = lax.axis_index("store")
    chosen = (owner_all == store_index)[..., None] & (
        position_all[..., None] == jnp.arange(capacity, dtype=jnp.int32)
    )
    outgoing_local = jnp.sum(chosen.astype(jnp.int32) * local_all[..., None], axis=1)
    filled_rows = jnp.any(chosen, axis=1)
    empty_value = jnp.zeros((), jnp.bfloat16)
    outgoing_shrink = jnp.where(
        filled_rows[..., None, None], shrink_matrices[outgoing_local], empty_value
    )
    outgoing_expand = jnp.where(
        filled_rows[..., None, None], expand_matrices[outgoing_local], empty_value
    )
    recv_a, recv_b = (
        lax.all_to_all(outgoing_shrink, "store", split_axis=0, concat_axis=0, tiled=True),
        lax.all_to_all(outgoing_expand, "store", split_axis=0, concat_axis=0, tiled=True),
    )
    owner_mine = slot_of // slots_per_holder
    position_mine = place_in_owner(owner_mine, store_count)
    flat_place = owner_mine * capacity + position_mine
    fetched_a = recv_a.reshape((store_count * capacity,) + recv_a.shape[2:])[flat_place]
    fetched_b = recv_b.reshape((store_count * capacity,) + recv_b.shape[2:])[flat_place]
    live_slot = block_slot_rows >= 0
    picked = jnp.where(
        live_slot[..., None],
        head_rows[jnp.maximum(block_slot_rows, 0)],
        jnp.zeros((), jnp.bfloat16),
    )
    shrink_part = jnp.einsum("bsh,brh->bsr", picked, fetched_a, preferred_element_type=jnp.float32)
    summed_shrink = lax.psum(shrink_part, "tensor")
    shrink_output = lax.dynamic_slice_in_dim(
        summed_shrink, lax.axis_index("tensor") * rank_portion, rank_portion, 2
    )
    shrink_output = shrink_output.astype(jnp.bfloat16)
    targets = jnp.where(live_slot, block_slot_rows, group_rows)
    block_ids = lax.broadcasted_iota(jnp.int32, block_slot_rows.shape, 0)
    row_shrink = (
        jnp.zeros((group_rows + 1, blocks_here, rank_portion), jnp.bfloat16)
        .at[targets, block_ids]
        .set(shrink_output)
    )
    row_shrink = row_shrink[:group_rows].reshape(group_rows, blocks_here * rank_portion)
    stacked_b = fetched_b.reshape(blocks_here * rank_portion, -1)
    summed = lax.psum_scatter(
        jnp.dot(head_rows, output_weight, preferred_element_type=jnp.float32)
        + ADAPTER_SCALE * jnp.dot(row_shrink, stacked_b, preferred_element_type=jnp.float32),
        "tensor",
        scatter_dimension=0,
        tiled=True,
    )
    return (hidden.astype(jnp.float32) + summed).astype(jnp.bfloat16)


def solution(mesh):
    in_specs = (
        P(("groups", "store", "tensor"), None),
        P(("groups", "store", "tensor"), None),
        P(("groups", "store", "tensor"), None, None, None),
        P(("groups", "store", "tensor"), None, None, None),
        P(("groups", "store", "tensor")),
        P("tensor", None),
        P(("groups", "store"), None, "tensor"),
        P(("groups", "store"), "tensor", None),
        P(("groups", "store"), None),
        P(("groups", "store")),
        P("groups"),
    )
    out_specs = P(("groups", "store", "tensor"), None)
    tensors, stores = mesh.shape["tensor"], mesh.shape["store"]

    def plan(*args):
        rows_dev, model = args[0].shape
        kv_heads = args[2].shape[1]
        fits = stores * tensors * rows_dev * model * 2 <= 4 * 1024 * 1024
        fits = fits and stores == 4 and rows_dev % 16 == 0 and kv_heads % tensors == 0
        return (rows_plan if fits else on_device)(*args)

    return jax.shard_map(
        plan, mesh=mesh, in_specs=in_specs, out_specs=out_specs, check_vma=False
    )
```
